32 devices in a mesh: groups: 2 (over x), dev: 8 (over z, y), tp: 2 (over core).
Axes of the slice: x: 2, y: 2, z: 4, core: 2. Of those that a mesh axis runs over, the one named last changes fastest.
Arguments:
- h_in: bfloat16 [256, 4096], P(('groups', 'dev')), parts along dimension 0, may hold values from -6 to 6
- query: bfloat16 [256, 8192], P(('groups', 'dev'), 'tp'), parts along dimension 0, may hold values from -200 to 200
- key_cache: bfloat16 [256, 128, 512], P(('groups', 'dev'), None, 'tp'), parts along dimension 0, may hold values from -8 to 8
- cached_value_rows: bfloat16 [256, 128, 512], P(('groups', 'dev'), None, 'tp'), parts along dimension 0, may hold values from -6 to 6
- fresh_token_key: bfloat16 [256, 512], P(('groups', 'dev'), 'tp'), parts along dimension 0, may hold values from -6 to 6
- fresh_token_value: bfloat16 [256, 512], P(('groups', 'dev'), 'tp'), parts along dimension 0, may hold values from -6 to 6
- lengths: int32 [256], P(('groups', 'dev')), parts along dimension 0, may hold values from 2 to 128, as said below
- routes: int32 [256, 2], P(('groups', 'dev')), parts along dimension 0, may hold values from 0 to 3, all different within a row; in each aligned block of 16 rows (0 to 15, 16 to 31, ...) at most 12 rows name the same one
- w_out: bfloat16 [8192, 4096], P('tp', 'dev'), may hold values from -0.0625 to 0.0625
- gain: bfloat16 [4096], replicated, may hold values from 0.099609375 to 1.8984375
- router_weight: bfloat16 [4096, 4], replicated, may hold values from -0.09375 to 0.09375
- w_gate: bfloat16 [8, 4096, 768], P('dev', None, 'tp'), may hold values from -0.09375 to 0.09375
- w_up: bfloat16 [8, 4096, 768], P('dev', None, 'tp'), may hold values from -0.09375 to 0.09375
- w_down: bfloat16 [8, 768, 4096], P('dev', 'tp'), may hold values from -0.15625 to 0.15625
Outputs:
- mixed: bfloat16 [256, 4096], P(('groups', 'dev'), 'tp'), parts along dimension 0
The draws below stay inside these ranges and needn't reach their ends.
There are 2 independent parts, one for each index of `groups`. The reference program is written for one: setup_inputs(seed, part) draws one part's arguments, and reference() takes and returns one part's arrays. A program takes and returns all parts, laid end to end along the dimension named above; an argument that names none is the same for every part. Nothing has to cross between parts.
Inputs may be any that keep to these rules, and one draw needn't show every extreme that they name: `routes`: within the 16 rows of one dev index no expert is named more than 12 times, a bound that some block reaches; each row names 2 different experts. `lengths`: some row uses all 128 slots.
All inputs are finite; a program needn't handle non-finite values.
Results may differ from the reference program's by a relative error of at most 0.0055.
Values may be sent and summed in bfloat16 or wider, within the bound.
A program may use at most 128 MiB of HBM per device.

```python
import math
import jax
import jax.numpy as jnp
import numpy as np
from jax import lax

D = 4096
QUERY_HEADS = 64
KEY_VALUE_HEADS = 4
HEAD_SIZE = 128
FF = 1536
HALVES = 2
ROWS_DEV = 16
CACHE_SLOT_COUNT = 128
EXPERTS = 4
TOPK = 2
CAP = 12
DECODE_ROWS = 128


def draw_query(key, part):
    key = jax.random.fold_in(key, 1)
    value_entries = jax.random.normal(key, (DECODE_ROWS, QUERY_HEADS, HEAD_SIZE), jnp.float32)
    value_entries = jnp.clip(value_entries, -6.0, 6.0)
    return value_entries.reshape(DECODE_ROWS, QUERY_HEADS * HEAD_SIZE).astype(jnp.bfloat16)


def draw_key_cache(key, part):
    key = jax.random.fold_in(key, 2)
    value_entries = jnp.clip(jax.random.normal(key, (DECODE_ROWS, CACHE_SLOT_COUNT, KEY_VALUE_HEADS, HEAD_SIZE), jnp.float32), -6.0, 6.0)
    return value_entries.reshape(DECODE_ROWS, CACHE_SLOT_COUNT, KEY_VALUE_HEADS * HEAD_SIZE).astype(jnp.bfloat16)


def draw_lengths(key, part):
    key = jax.random.fold_in(key, 3)
    counts = jax.random.randint(key, (DECODE_ROWS,), 2, CACHE_SLOT_COUNT + 1)
    chosen = jax.random.randint(jax.random.fold_in(key, 7), (), 0, DECODE_ROWS)
    return counts.at[chosen].set(CACHE_SLOT_COUNT)


def level_of(key, shape, split, least, high):
    def one(axis_at, shards_of):
        steps = jax.random.uniform(jax.random.fold_in(jax.random.fold_in(key, 6), axis_at), (shards_of,), jnp.float32, least / len(split), high / len(split))
        return jnp.repeat(jnp.exp(steps), shape[axis_at] // shards_of).reshape((-1,) + (1,) * (len(shape) - axis_at - 1))

    loudness = one(*split[0])
    for cut in split[1:]:
        loudness = loudness * one(*cut)
    return loudness


def deal_out(key, own, number, rows, number_of, top, most, lean):
    ranking = jax.random.permutation(key, number_of)
    crowded, ordinary = shares(number_of, rows * top, most, lean, True), shares(number_of, rows * top, most, lean, False)
    places = jnp.arange(number_of)

    def named(sizes, offset_by):
        used = int((sizes > 0).sum())
        fixed = max(1, used // 4)
        passed = fixed + (places - fixed + offset_by * (used - fixed)) % max(1, number_of - fixed)
        return jnp.zeros((number_of,), jnp.int32).at[ranking[jnp.where(places < fixed, places, passed)]].set(jnp.asarray(sizes, jnp.int32))

    sizes = jnp.where(number % 4 == 0, named(crowded, number // 4), named(ordinary, number - number // 4 - 1))
    mixed = jax.random.permutation(jax.random.fold_in(own, 3), number_of)
    giver, sink = mixed[0:number_of // 2 * 2:2], mixed[1:number_of // 2 * 2:2]
    slack = jnp.minimum(sizes[giver] - 1, most - sizes[sink]) // 2
    slack = jnp.where((giver == ranking[0]) | (sink == ranking[0]) | (sizes[sink] == 0), 0, jnp.maximum(slack, 0))
    passed = jax.random.randint(jax.random.fold_in(own, 4), (number_of // 2,), 0, 1 << 20) % (slack + 1)
    sizes = sizes.at[giver].add(-passed).at[sink].add(passed)
    members = jnp.searchsorted(jnp.cumsum(sizes), jnp.arange(rows * top), side="right").astype(jnp.int32)
    table = members.reshape(top, rows).T
    table = table[jax.random.permutation(jax.random.fold_in(own, 1), rows)]
    offset_by = jax.random.randint(jax.random.fold_in(own, 2), (rows, 1), 0, top)
    return jnp.take_along_axis(table, (jnp.arange(top)[None, :] + offset_by) % top, axis=1)


def shares(amount, total, bound, skew, full):
    loads = [(1 << 20) // math.isqrt(rank ** skew) + 1 for rank in range(1, amount + 1)]
    largest = bound if full else min(bound, max(-(-total // amount), total * loads[0] // sum(loads)))
    least = 1 if total - largest >= amount - 1 else 0
    given, rest = [largest] + [least] * (amount - 1), total - largest - least * (amount - 1)
    while rest > 0:
        free = [i for i in range(1, amount) if given[i] < largest] or [i for i in range(1, amount) if given[i] < bound]
        mass, budget = sum([loads[i] for i in free]), rest
        for i in free:
            extra = min(bound - given[i], max(1, budget * loads[i] // mass), rest)
            given[i] = given[i] + extra
            rest = rest - extra
    return np.array(given)


def normal_values(key, dims, spread, most, split=(), kind=jnp.bfloat16):
    level = level_of(key, dims, split, -0.22, 0.18) if split else 1.0
    values = jax.random.normal(key, dims, jnp.float32) * spread * level
    return jnp.minimum(jnp.maximum(values, -most), most).astype(kind)


def setup_inputs(seed: int = 0, part: int = 0) -> dict:
    keys = jax.random.split(jax.random.key(seed), 15)
    own_keys = jax.random.split(jax.random.fold_in(keys[14], part), 15)
    h_in = normal_values(own_keys[0], (DECODE_ROWS, D), 1.0, 6.0, ((0, 8),))
    query = draw_query(jax.random.fold_in(jax.random.fold_in(keys[14], part), 71), part)
    key_cache = draw_key_cache(jax.random.fold_in(jax.random.fold_in(keys[14], part), 71), part)
    cached_value_rows = normal_values(own_keys[3], (DECODE_ROWS, CACHE_SLOT_COUNT, KEY_VALUE_HEADS * HEAD_SIZE), 1.0, 6.0, ((0, 8), (2, 2)))
    fresh_token_key = normal_values(own_keys[4], (DECODE_ROWS, KEY_VALUE_HEADS * HEAD_SIZE), 1.0, 6.0, ((0, 8), (1, 2)))
    fresh_token_value = normal_values(own_keys[5], (DECODE_ROWS, KEY_VALUE_HEADS * HEAD_SIZE), 1.0, 6.0, ((0, 8), (1, 2)))
    lengths = draw_lengths(jax.random.fold_in(jax.random.fold_in(keys[14], part), 71), part)
    routes_keys = jax.random.split(jax.random.fold_in(own_keys[7], 1), DECODE_ROWS // ROWS_DEV)
    routes_turns = jax.random.permutation(jax.random.fold_in(own_keys[7], 3), DECODE_ROWS // ROWS_DEV)
    routes = jax.vmap(lambda own, number: deal_out(jax.random.fold_in(own_keys[7], 2), own, number, ROWS_DEV, EXPERTS, TOPK, CAP, 2))(routes_keys, routes_turns).reshape((DECODE_ROWS, TOPK))
    w_out = normal_values(keys[8], (QUERY_HEADS * HEAD_SIZE, D), (QUERY_HEADS * HEAD_SIZE) ** -0.5, 0.0625, ((0, 2), (1, 8)))
    gain = jnp.clip(1.0 + 0.18 * jax.random.normal(keys[9], (D,), jnp.float32), 0.099609375, 1.8984375).astype(jnp.bfloat16)
    router_weight = normal_values(keys[10], (D, EXPERTS), D ** -0.5, 0.09375)
    w_gate = normal_values(keys[11], (HALVES * EXPERTS, D, FF // HALVES), D ** -0.5, 0.09375, ((0, 8), (2, 2)))
    w_up = normal_values(keys[12], (HALVES * EXPERTS, D, FF // HALVES), D ** -0.5, 0.09375, ((0, 8), (2, 2)))
    w_down = normal_values(keys[13], (HALVES * EXPERTS, FF // HALVES, D), FF ** -0.5, 0.15625, ((0, 8), (1, 2)))
    return dict(h_in=h_in, query=query, key_cache=key_cache, cached_value_rows=cached_value_rows, fresh_token_key=fresh_token_key, fresh_token_value=fresh_token_value, lengths=lengths, routes=routes, w_out=w_out, gain=gain, router_weight=router_weight, w_gate=w_gate, w_up=w_up, w_down=w_down)


epsilon = 1e-06

def attend(query, key_cache, cached_value_rows, fresh_token_key, fresh_token_value, lengths):
    count = query.shape[0]
    slots = key_cache.shape[1]
    kv_heads = key_cache.shape[2] // HEAD_SIZE
    queries = query.reshape(count, kv_heads, -1, HEAD_SIZE).astype(jnp.float32)
    keys_old = key_cache.reshape(count, slots, kv_heads, HEAD_SIZE).astype(jnp.float32)
    values_old = cached_value_rows.reshape(count, slots, kv_heads, HEAD_SIZE).astype(jnp.float32)
    keys_new = fresh_token_key.reshape(count, kv_heads, HEAD_SIZE).astype(jnp.float32)
    values_new = fresh_token_value.reshape(count, kv_heads, HEAD_SIZE).astype(jnp.float32)
    factor = 1.0 / math.sqrt(HEAD_SIZE)
    scores = jnp.einsum('rgqd,rcgd->rgqc', queries, keys_old) * factor
    score_new = jnp.einsum('rgqd,rgd->rgq', queries, keys_new) * factor
    positions = jnp.arange(slots, dtype=jnp.int32)
    live = (positions[None, :] < lengths[:, None])[:, None, None, :]
    scores = jnp.where(live, scores, -1e+30)
    highest = jnp.maximum(lax.optimization_barrier(jnp.max(scores, -1)), score_new)
    expo = jnp.where(live, jnp.exp(scores - highest[..., None]), 0.0)
    expo_new = jnp.exp(score_new - highest)
    total = lax.optimization_barrier(jnp.sum(expo, -1)) + expo_new
    weights = lax.optimization_barrier((expo / total[..., None]).astype(jnp.bfloat16)).astype(jnp.float32)
    weight_new = lax.optimization_barrier((expo_new / total).astype(jnp.bfloat16)).astype(jnp.float32)
    blended = jnp.einsum('rgqc,rcgd->rgqd', weights, values_old) + weight_new[..., None] * values_new[:, :, None, :]
    return blended.astype(jnp.bfloat16).reshape(count, -1)

def reference(h_in, query, key_cache, cached_value_rows, fresh_token_key, fresh_token_value, lengths, routes, w_out, gain, router_weight, w_gate, w_up, w_down):
    attn = attend(query, key_cache, cached_value_rows, fresh_token_key, fresh_token_value, lengths)
    h_one = h_in.astype(jnp.float32) + jnp.dot(attn, w_out, preferred_element_type=jnp.float32)
    scale_rows = lax.rsqrt(lax.optimization_barrier(jnp.mean(h_one * h_one, 1)) + epsilon)
    normed = (h_one * scale_rows[:, None] * gain.astype(jnp.float32)[None, :]).astype(jnp.bfloat16)
    logits = jnp.dot(normed, router_weight, preferred_element_type=jnp.float32)
    picked = jnp.take_along_axis(logits, routes, 1)
    expo = jnp.exp(picked)
    gates = expo / lax.optimization_barrier(jnp.sum(expo, 1, keepdims=True))
    experts_all = router_weight.shape[1]

    def one_expert(carry, index):
        gate_cols = jnp.concatenate([w_gate[index], w_gate[index + experts_all]], 1)
        up_cols = jnp.concatenate([w_up[index], w_up[index + experts_all]], 1)
        down_rows = jnp.concatenate([w_down[index], w_down[index + experts_all]], 0)
        gated = jnp.dot(normed, gate_cols, preferred_element_type=jnp.float32)
        upper = jnp.dot(normed, up_cols, preferred_element_type=jnp.float32)
        act = (jax.nn.silu(gated) * upper).astype(jnp.bfloat16)
        result = jnp.dot(act, down_rows, preferred_element_type=jnp.float32)
        weight = lax.optimization_barrier(jnp.sum(jnp.where(routes == index, gates, 0.0), 1))
        return (carry + weight[:, None] * result, None)
    moe, _ = lax.scan(one_expert, jnp.zeros(h_one.shape, jnp.float32), jnp.arange(experts_all, dtype=jnp.int32))
    return (h_one + moe).astype(jnp.bfloat16)
```

```python
import functools
import math

import jax
import jax.numpy as jnp
from jax import lax
from jax.experimental import pallas as pl
from jax.experimental.pallas import tpu as pltpu
from jax.sharding import PartitionSpec as P

HEAD = 128
EPS = 1e-06
F32 = jnp.float32
BF16 = jnp.bfloat16
NT = (((1,), (1,)), ((), ()))


def layer_kernel(
    n, experts,
    len_ref, h_ref, q_ref, fk_ref, fv_ref, routes_ref, gain_ref, rw_ref,
    kc_hbm, vc_hbm, wo_hbm, wg_hbm, wu_hbm, wd_hbm,
    out_ref,
    kc, vc, wo, wg, wu, wd,
    qs, fkf, fvf, sc, pn, pw, ob,
    ag, pacc, pbuf, pr, h1, xg, act, ysib, yin, yacc, sbuf, rbuf,
    lsem, ag_s, ag_r, af_s, af_r, p_s, p_r, ps_s, ps_r,
    x_s, x_r, xf_s, xf_r, xs_s, xs_r, y_s, y_r, m_s, m_r,
):
    d = lax.axis_index("dev")
    c = lax.axis_index("tp")
    tp = 2
    cols = n // 2
    a = d // 2
    b = d % 2
    twin = a * 2 + (1 - b)
    rows = q_ref.shape[0]
    width = h_ref.shape[1]
    half = width // tp
    kvh = fk_ref.shape[1] // HEAD
    heads = q_ref.shape[1] // HEAD
    per = heads // kvh
    kpart = per * HEAD
    cw = wo.shape[1]
    ep = rw_ref.shape[0] // 2

    local = [
        pltpu.make_async_copy(src, dst, lsem.at[i])
        for i, (src, dst) in enumerate(
            [(kc_hbm, kc), (vc_hbm, vc), (wo_hbm, wo), (wg_hbm.at[0], wg), (wu_hbm.at[0], wu), (wd_hbm.at[0], wd)]
        )
    ]
    for cp in local:
        cp.start()

    barrier = pltpu.get_barrier_semaphore()
    for k in range(1, n):
        pl.semaphore_signal(
            barrier, inc=1, device_id={"dev": lax.rem(d + k, n)}, device_id_type=pl.DeviceIdType.MESH
        )
    pl.semaphore_signal(barrier, inc=1, device_id={"tp": 1 - c}, device_id_type=pl.DeviceIdType.MESH)

    def send(src, dst, ssem, rsem, **to):
        cp = pltpu.make_async_remote_copy(
            src_ref=src, dst_ref=dst, send_sem=ssem, recv_sem=rsem,
            device_id=to, device_id_type=pl.DeviceIdType.MESH,
        )
        cp.start()
        return cp

    pending = []

    for hh in range(heads):
        qs[pl.ds(hh, rows, stride=heads), :] = q_ref[:, hh * HEAD:(hh + 1) * HEAD].astype(F32)
    for g in range(kvh):
        fkf[g] = fk_ref[:, g * HEAD:(g + 1) * HEAD].astype(F32)
        fvf[g] = fv_ref[:, g * HEAD:(g + 1) * HEAD].astype(F32)
    factor = 1.0 / math.sqrt(HEAD)
    local[0].wait()
    slots = kc.shape[1]
    lane = lax.broadcasted_iota(jnp.int32, (per, slots), 1)
    step = 4

    @pl.loop(0, rows, step=step)
    def _(r0):
        for i in range(step):
            r = r0 + i
            live = lane < len_ref[r]
            for g in range(kvh):
                at = pl.ds(pl.multiple_of(r * heads + g * per, per), per)
                q = qs[at, :]
                s = lax.dot_general(
                    q.astype(BF16), kc[r, :, g * HEAD:(g + 1) * HEAD], NT, preferred_element_type=F32
                )
                sc[at, :] = jnp.where(live, s * factor, -1e30)
                pn[at, :] = q * fkf[g, pl.ds(r, 1), :]

    chunk = 128

    @pl.loop(0, rows * heads, step=chunk)
    def _(r0):
        at = pl.ds(pl.multiple_of(r0, chunk), chunk)
        s = sc[at, :]
        sn = jnp.sum(pn[at, :], -1, keepdims=True) * factor
        m = jnp.maximum(jnp.max(s, -1, keepdims=True), sn)
        p = jnp.exp(s - m)
        en = jnp.exp(sn - m)
        tot = jnp.sum(p, -1, keepdims=True) + en
        pw[at, :] = (p / tot).astype(BF16)
        pn[at, :] = jnp.broadcast_to((en / tot).astype(BF16).astype(F32), (chunk, HEAD))

    local[1].wait()

    @pl.loop(0, rows, step=step)
    def _(r0):
        for i in range(step):
            r = r0 + i
            for g in range(kvh):
                at = pl.ds(pl.multiple_of(r * heads + g * per, per), per)
                o = jnp.dot(pw[at, :], vc[r, :, g * HEAD:(g + 1) * HEAD], preferred_element_type=F32)
                ob[at, :] = o + pn[at, :] * fvf[g, pl.ds(r, 1), :]

    pl.semaphore_wait(barrier, n)

    sent = []
    for g in range(kvh):
        for hh in range(per):
            ag[g, d, :, hh * HEAD:(hh + 1) * HEAD] = ob[
                pl.ds(g * per + hh, rows, stride=heads), :
            ].astype(BF16)
        blk = ag.at[g, d]
        one = [send(blk, blk, af_s.at[g, 0], af_r.at[g, 0], dev=twin)]
        for k in range(1, cols):
            j = lax.rem(a + k, cols) * 2 + b
            one.append(send(blk, blk, ag_s.at[g, k], ag_r.at[g, k], dev=j))
        sent.append(one)
    fwd = []
    for g in range(kvh):
        for k in range(1, cols):
            sent[g][k].wait_recv()
            src = lax.rem(a + cols - k, cols) * 2 + b
            blk = ag.at[g, src]
            fwd.append(send(blk, blk, af_s.at[g, k], af_r.at[g, k], dev=twin))
    local[2].wait()
    blocks = min(n, 128 // rows)
    mrows = blocks * rows
    for g in range(kvh):
        sent[g][0].wait_recv()
        for k in range(1, cols):
            fwd[g * (cols - 1) + k - 1].wait_recv()

        @pl.loop(0, n, step=blocks)
        def _(j0):
            x = ag[g, pl.ds(j0, blocks)].reshape(mrows, kpart)
            y = jnp.dot(x, wo[g * kpart:(g + 1) * kpart, :], preferred_element_type=F32)
            y = y.reshape(blocks, rows, cw)
            if g == 0:
                pacc[pl.ds(j0, blocks)] = y
            else:
                y = y + pacc[pl.ds(j0, blocks)]
                pacc[pl.ds(j0, blocks)] = y
            if g == kvh - 1:
                pbuf[pl.ds(j0, blocks)] = y.astype(BF16)
    for one in sent:
        pending += one
    pending += fwd

    hops = []
    for k in range(1, n):
        j = lax.rem(d + k, n)
        hops.append(send(pbuf.at[j], pr.at[c, d], p_s.at[k], p_r.at[k], dev=j))
    pr[c, d] = pbuf[d]
    sib = [send(pr.at[c, d], pr.at[c, d], ps_s.at[0], ps_r.at[0], tp=1 - c)]
    for k in range(1, n):
        hops[k - 1].wait_recv()
        src = lax.rem(d + n - k, n)
        sib.append(send(pr.at[c, src], pr.at[c, src], ps_s.at[k], ps_r.at[k], tp=1 - c))
    for cp in sib:
        cp.wait_recv()
    pending += hops + sib

    ss = jnp.zeros((rows, 1), F32)
    for j in range(n):
        at = slice(j * cw, (j + 1) * cw)
        v = h_ref[:, at].astype(F32) + (pr[0, j].astype(F32) + pr[1, j].astype(F32))
        h1[:, at] = v
        ss = ss + jnp.sum(v * v, -1, keepdims=True)
    scale = lax.rsqrt(ss / width + EPS)
    logits = jnp.zeros((rows, 2 * ep), F32)
    for t in range(tp):
        at = slice(t * half, (t + 1) * half)
        x2 = (h1[:, at] * scale * gain_ref[:, at].astype(F32)).astype(BF16)
        xg[t, d, :, 0:half] = x2
        logits = logits + lax.dot_general(x2, rw_ref[:, at], NT, preferred_element_type=F32)
    spot = lax.broadcasted_iota(jnp.int32, (rows, 2 * ep), 1)
    expert = jnp.where(spot >= ep, spot - ep, spot)
    chosen = jnp.zeros((rows, 2 * ep), jnp.bool_)
    for k in range(routes_ref.shape[1]):
        chosen = chosen | (expert == routes_ref[:, k:k + 1])
    expo = jnp.where(chosen, jnp.exp(logits), 0.0)
    gates = expo / jnp.sum(jnp.where(spot < ep, expo, 0.0), -1, keepdims=True)
    high = gates.astype(BF16).astype(F32)
    ext = jnp.where(spot < ep, high, gates - high).astype(BF16)
    for t in range(tp):
        xg[t, d, :, half:half + HEAD] = jnp.zeros((rows, HEAD), BF16)
        xg[t, d, :, half:half + 2 * ep] = ext

    blk = xg.at[c, d]
    first = [send(blk, blk, xf_s.at[0], xf_r.at[0], dev=twin)]
    for k in range(1, cols):
        j = lax.rem(a + k, cols) * 2 + b
        first.append(send(blk, blk, x_s.at[k], x_r.at[k], dev=j))
    sib = []
    xfw = []
    for k in range(1, cols):
        first[k].wait_recv()
        src = lax.rem(a + cols - k, cols) * 2 + b
        blk = xg.at[c, src]
        xfw.append(send(blk, blk, xf_s.at[k], xf_r.at[k], dev=twin))
        sib.append(send(blk, blk, xs_s.at[k], xs_r.at[k], tp=1 - c))
    for k in range(cols):
        (first[0] if k == 0 else xfw[k - 1]).wait_recv()
        src = lax.rem(a + cols - k, cols) * 2 + (1 - b)
        blk = xg.at[c, src]
        sib.append(send(blk, blk, xs_s.at[cols + k], xs_r.at[cols + k], tp=1 - c))
    for cp in sib:
        cp.wait_recv()
    pending += first + xfw + sib

    local[3].wait()
    local[4].wait()
    local[5].wait()
    mine = lax.rem(d, experts)
    other = pl.multiple_of((1 - c) * half, half)
    own = pl.multiple_of(c * half, half)

    @pl.loop(0, n, step=blocks)
    def _(j0):
        x0 = xg[0, pl.ds(j0, blocks), :, 0:half].reshape(mrows, half)
        x1 = xg[1, pl.ds(j0, blocks), :, 0:half].reshape(mrows, half)
        gt = jnp.dot(x0, wg[0:half, :], preferred_element_type=F32)
        gt = gt + jnp.dot(x1, wg[half:, :], preferred_element_type=F32)
        up = jnp.dot(x0, wu[0:half, :], preferred_element_type=F32)
        up = up + jnp.dot(x1, wu[half:, :], preferred_element_type=F32)
        act[pl.ds(j0, blocks)] = (
            (gt / (1.0 + jnp.exp(-gt)) * up).astype(BF16).reshape(blocks, rows, act.shape[2])
        )

    def weight_of(j0):
        e = xg[0, pl.ds(j0, blocks), :, half:half + HEAD].reshape(mrows, HEAD).astype(F32)
        ln = lax.broadcasted_iota(jnp.int32, (mrows, HEAD), 1)
        return jnp.sum(jnp.where((ln == mine) | (ln == mine + ep), e, 0.0), -1, keepdims=True)

    @pl.loop(0, n, step=blocks)
    def _(j0):
        w = weight_of(j0)
        x = act[pl.ds(j0, blocks)].reshape(mrows, act.shape[2])
        y = jnp.dot(x, wd[:, pl.ds(other, half)], preferred_element_type=F32) * w
        ysib[pl.ds(j0, blocks)] = y.astype(BF16).reshape(blocks, rows, half)

    ycp = send(ysib, yin, y_s, y_r, tp=1 - c)

    @pl.loop(0, n, step=blocks)
    def _(j0):
        w = weight_of(j0)
        x = act[pl.ds(j0, blocks)].reshape(mrows, act.shape[2])
        y = jnp.dot(x, wd[:, pl.ds(own, half)], preferred_element_type=F32) * w
        yacc[pl.ds(j0, blocks)] = y.reshape(blocks, rows, half)

    ycp.wait_recv()
    hops = []
    for k in range(1, n):
        j = lax.rem(d + k, n)
        sbuf[j] = (yacc[j] + yin[j].astype(F32)).astype(BF16)
        hops.append(send(sbuf.at[j], rbuf.at[k], m_s.at[k], m_r.at[k], dev=j))
    total = h1[:, pl.ds(own, half)] + (yacc[d] + yin[d].astype(F32))
    for k in range(1, n):
        hops[k - 1].wait_recv()
        total = total + rbuf[k].astype(F32)
    out_ref[...] = total.astype(BF16)
    pending += [ycp] + hops
    for cp in pending:
        cp.wait_send()


def shards(
    n, h_in, query, key_cache, cached_value_rows, fresh_token_key, fresh_token_value,
    lengths, routes, w_out, gain, router_weight, w_gate, w_up, w_down,
):
    rows, width = h_in.shape
    experts = router_weight.shape[1]
    ep = -(-experts // 16) * 16
    rw = jnp.pad(router_weight.T, ((0, ep - experts), (0, 0)))
    rw = jnp.concatenate([rw, rw], 0)
    half = width // 2
    kvh = fresh_token_key.shape[1] // HEAD
    heads = query.shape[1] // HEAD
    per = heads // kvh
    cw = w_out.shape[1]
    ff = w_gate.shape[2]
    cols = n // 2
    slots = key_cache.shape[1]
    vm = pl.BlockSpec(memory_space=pltpu.VMEM)
    anyw = pl.BlockSpec(memory_space=pl.ANY)
    dma = pltpu.SemaphoreType.DMA
    return pl.pallas_call(
        functools.partial(layer_kernel, n, experts),
        out_shape=jax.ShapeDtypeStruct((rows, half), BF16),
        in_specs=[pl.BlockSpec(memory_space=pltpu.SMEM)] + [vm] * 7 + [anyw] * 6,
        out_specs=vm,
        scratch_shapes=[
            pltpu.VMEM(key_cache.shape, BF16),
            pltpu.VMEM(cached_value_rows.shape, BF16),
            pltpu.VMEM(w_out.shape, BF16),
            pltpu.VMEM(w_gate.shape[1:], BF16),
            pltpu.VMEM(w_up.shape[1:], BF16),
            pltpu.VMEM(w_down.shape[1:], BF16),
            pltpu.VMEM((rows * heads, HEAD), F32),
            pltpu.VMEM((kvh, rows, HEAD), F32),
            pltpu.VMEM((kvh, rows, HEAD), F32),
            pltpu.VMEM((rows * heads, slots), F32),
            pltpu.VMEM((rows * heads, HEAD), F32),
            pltpu.VMEM((rows * heads, slots), BF16),
            pltpu.VMEM((rows * heads, HEAD), F32),
            pltpu.VMEM((kvh, n, rows, per * HEAD), BF16),
            pltpu.VMEM((n, rows, cw), F32),
            pltpu.VMEM((n, rows, cw), BF16),
            pltpu.VMEM((2, n, rows, cw), BF16),
            pltpu.VMEM((rows, width), F32),
            pltpu.VMEM((2, n, rows, half + HEAD), BF16),
            pltpu.VMEM((n, rows, ff), BF16),
            pltpu.VMEM((n, rows, half), BF16),
            pltpu.VMEM((n, rows, half), BF16),
            pltpu.VMEM((n, rows, half), F32),
            pltpu.VMEM((n, rows, half), BF16),
            pltpu.VMEM((n, rows, half), BF16),
            dma((6,)),
            dma((kvh, cols)), dma((kvh, cols)), dma((kvh, cols)), dma((kvh, cols)),
            dma((n,)), dma((n,)), dma((n,)), dma((n,)),
            dma((cols,)), dma((cols,)), dma((cols,)), dma((cols,)), dma((n,)), dma((n,)),
            dma, dma, dma((n,)), dma((n,)),
        ],
        compiler_params=pltpu.CompilerParams(
            collective_id=0, has_side_effects=True, vmem_limit_bytes=60 * 1024 * 1024
        ),
    )(
        lengths, h_in, query, fresh_token_key, fresh_token_value, routes, gain[None, :], rw,
        key_cache, cached_value_rows, w_out, w_gate, w_up, w_down,
    )


def solution(mesh):
    placed = (
        P(("groups", "dev"), None),
        P(("groups", "dev"), "tp"),
        P(("groups", "dev"), None, "tp"),
        P(("groups", "dev"), None, "tp"),
        P(("groups", "dev"), "tp"),
        P(("groups", "dev"), "tp"),
        P(("groups", "dev")),
        P(("groups", "dev"), None),
        P("tp", "dev"),
        P(),
        P(),
        P("dev", None, "tp"),
        P("dev", None, "tp"),
        P("dev", "tp", None),
    )
    return jax.shard_map(
        functools.partial(shards, mesh.shape["dev"]),
        mesh=mesh, in_specs=placed, out_specs=P(("groups", "dev"), "tp"), check_vma=False,
    )
```

```python
import functools
import math

import jax
import jax.numpy as jnp
from jax import lax
from jax.experimental import pallas as pl
from jax.experimental.pallas import tpu as pltpu
from jax.sharding import PartitionSpec as P

HEAD = 128
EPS = 1e-06
F32 = jnp.float32
BF16 = jnp.bfloat16
NT = (((1,), (1,)), ((), ()))


def layer_kernel(
    n, experts,
    len_ref, routes_ref, h_ref, q_ref, fk_ref, fv_ref, gain_ref, rw_ref,
    kc_hbm, vc_hbm, wo_hbm, wg_hbm, wu_hbm, wd_hbm,
    out_ref,
    kc, vc, wo, wg, wu, wd, rw,
    qs, fkf, fvf, sc, pn, pw, ob,
    ag, pbuf, pr, h1, xg, act, ysib, yin, yacc, sbuf, rbuf,
    lsem, a_s, a_r, p_s, p_r, ps_s, ps_r, x_s, x_r, xs_s, xs_r, y_s, y_r, m_s, m_r,
):
    d = lax.axis_index("dev")
    c = lax.axis_index("tp")
    hops = n // 2
    rows = q_ref.shape[0]
    width = h_ref.shape[1]
    half = width // 2
    quart = half // 2
    kvh = fk_ref.shape[1] // HEAD
    heads = q_ref.shape[1] // HEAD
    per = heads // kvh
    kpart = per * HEAD
    cw = wo.shape[1]
    ep = rw.shape[0] // 2

    odd = lax.rem(d, 2)
    pos = (1 - odd) * lax.div(d, 2) + odd * (n - 1 - lax.div(d, 2))

    def at_pos(k):
        p = lax.rem(pos + (k % n), n)
        back = lax.div(p, hops)
        return (1 - back) * 2 * p + back * (2 * (n - 1 - p) + 1)

    ahead = (at_pos(1), at_pos(-1))

    def limit(way, part):
        return hops if way == part else hops - 1

    def origin(way, step):
        return at_pos(-step if way == 0 else step)

    local = [
        pltpu.make_async_copy(src, dst, lsem.at[i])
        for i, (src, dst) in enumerate(
            [(kc_hbm, kc), (vc_hbm, vc), (wo_hbm, wo), (wg_hbm.at[0], wg), (wu_hbm.at[0], wu), (wd_hbm.at[0], wd)]
        )
    ]
    local[0].start()
    local[1].start()

    barrier = pltpu.get_barrier_semaphore()
    for k in range(1, n):
        pl.semaphore_signal(
            barrier, inc=1, device_id={"dev": lax.rem(d + k, n)}, device_id_type=pl.DeviceIdType.MESH
        )
    pl.semaphore_signal(barrier, inc=1, device_id={"tp": 1 - c}, device_id_type=pl.DeviceIdType.MESH)

    def send(src, dst, ssem, rsem, **to):
        cp = pltpu.make_async_remote_copy(
            src_ref=src, dst_ref=dst, send_sem=ssem, recv_sem=rsem,
            device_id=to, device_id_type=pl.DeviceIdType.MESH,
        )
        cp.start()
        return cp

    pending = []

    for hh in range(heads):
        qs[pl.ds(hh, rows, stride=heads), :] = q_ref[:, hh * HEAD:(hh + 1) * HEAD].astype(F32)
    for g in range(kvh):
        fkf[g] = fk_ref[:, g * HEAD:(g + 1) * HEAD].astype(F32)
        fvf[g] = fv_ref[:, g * HEAD:(g + 1) * HEAD].astype(F32)
    rw[...] = jnp.zeros(rw.shape, BF16)
    rw[0:experts, :] = rw_ref[...]
    rw[ep:ep + experts, :] = rw_ref[...]
    factor = 1.0 / math.sqrt(HEAD)
    slots = kc.shape[1]
    lane = lax.broadcasted_iota(jnp.int32, (per, slots), 1)
    step = 4
    chunk = 128
    moves = {}
    for g in range(kvh):
        if g == 0:
            local[0].wait()
            local[2].start()

        @pl.loop(0, rows, step=step)
        def _(r0):
            for i in range(step):
                r = r0 + i
                live = lane < len_ref[r]
                q = qs[pl.ds(pl.multiple_of(r * heads + g * per, per), per), :]
                at = pl.ds(pl.multiple_of(r * per, per), per)
                s = lax.dot_general(
                    q.astype(BF16), kc[r, :, g * HEAD:(g + 1) * HEAD], NT, preferred_element_type=F32
                )
                sc[at, :] = jnp.where(live, s * factor, -1e30)
                pn[at, :] = q * fkf[g, pl.ds(r, 1), :]

        @pl.loop(0, rows * per, step=chunk)
        def _(r0):
            at = pl.ds(pl.multiple_of(r0, chunk), chunk)
            s = sc[at, :]
            sn = jnp.sum(pn[at, :], -1, keepdims=True) * factor
            m = jnp.maximum(jnp.max(s, -1, keepdims=True), sn)
            p = jnp.exp(s - m)
            en = jnp.exp(sn - m)
            tot = jnp.sum(p, -1, keepdims=True) + en
            pw[at, :] = (p / tot).astype(BF16)
            pn[at, :] = jnp.broadcast_to((en / tot).astype(BF16).astype(F32), (chunk, HEAD))

        if g == 0:
            local[1].wait()
            for i in (3, 4, 5):
                local[i].start()

        @pl.loop(0, rows, step=step)
        def _(r0):
            for i in range(step):
                r = r0 + i
                at = pl.ds(pl.multiple_of(r * per, per), per)
                o = jnp.dot(pw[at, :], vc[r, :, g * HEAD:(g + 1) * HEAD], preferred_element_type=F32)
                ob[at, :] = o + pn[at, :] * fvf[g, pl.ds(r, 1), :]

        for hh in range(per):
            ag[g, d, :, hh * HEAD:(hh + 1) * HEAD] = ob[pl.ds(hh, rows, stride=per), :].astype(BF16)
        if g == 0:
            pl.semaphore_wait(barrier, n)
        blk = ag.at[g, d]
        for way in range(2):
            moves[way, g, 1] = send(blk, blk, a_s.at[way, g, 1], a_r.at[way, g, 1], dev=ahead[way])

    for st in range(1, hops + 1):
        for g in range(kvh):
            for way in range(2):
                top = limit(way, g % 2)
                if st <= top:
                    moves[way, g, st].wait_recv()
                if st < top:
                    blk = ag.at[g, origin(way, st)]
                    moves[way, g, st + 1] = send(
                        blk, blk, a_s.at[way, g, st + 1], a_r.at[way, g, st + 1], dev=ahead[way]
                    )
    pending += list(moves.values())
    local[2].wait()
    blocks = min(n, 128 // rows)
    mrows = blocks * rows

    @pl.loop(0, n, step=blocks)
    def _(j0):
        y = jnp.zeros((mrows, cw), F32)
        for g in range(kvh):
            x = ag[g, pl.ds(j0, blocks)].reshape(mrows, kpart)
            y = y + jnp.dot(x, wo[g * kpart:(g + 1) * kpart, :], preferred_element_type=F32)
        pbuf[pl.ds(j0, blocks)] = y.astype(BF16).reshape(blocks, rows, cw)

    out = []
    for k in range(1, n):
        j = lax.rem(d + k, n)
        out.append(send(pbuf.at[j], pr.at[c, d], p_s.at[k], p_r.at[k], dev=j))
    pr[c, d] = pbuf[d]
    sib = [send(pr.at[c, d], pr.at[c, d], ps_s.at[0], ps_r.at[0], tp=1 - c)]
    for k in range(1, n):
        out[k - 1].wait_recv()
        src = lax.rem(d + n - k, n)
        sib.append(send(pr.at[c, src], pr.at[c, src], ps_s.at[k], ps_r.at[k], tp=1 - c))
    for cp in sib:
        cp.wait_recv()
    pending += out + sib

    ss = jnp.zeros((rows, 1), F32)
    for j in range(n):
        at = slice(j * cw, (j + 1) * cw)
        v = h_ref[:, at].astype(F32) + (pr[0, j].astype(F32) + pr[1, j].astype(F32))
        h1[:, at] = v
        ss = ss + jnp.sum(v * v, -1, keepdims=True)
    scale = lax.rsqrt(ss / width + EPS)
    gain = gain_ref[...].astype(F32)
    for i in range(width // HEAD):
        x2 = (h1[:, i * HEAD:(i + 1) * HEAD] * scale * gain[i:i + 1, :]).astype(BF16)
        part, lo = divmod(i * HEAD, quart)
        xg[part, d, :, lo:lo + HEAD] = x2
    logits = jnp.zeros((rows, 2 * ep), F32)
    for part in range(4):
        logits = logits + lax.dot_general(
            xg[part, d, :, 0:quart], rw[:, part * quart:(part + 1) * quart], NT, preferred_element_type=F32
        )
    spot = lax.broadcasted_iota(jnp.int32, (rows, 2 * ep), 1)
    line = lax.broadcasted_iota(jnp.int32, (rows, 2 * ep), 0)
    expert = jnp.where(spot >= ep, spot - ep, spot)
    chosen = jnp.zeros((rows, 2 * ep), jnp.bool_)
    for k in range(routes_ref.shape[0]):
        named = jnp.zeros((rows, 2 * ep), jnp.int32)
        for r in range(rows):
            named = jnp.where(line == r, routes_ref[k, r], named)
        chosen = chosen | (expert == named)
    expo = jnp.where(chosen, jnp.exp(logits), 0.0)
    gates = expo / jnp.sum(jnp.where(spot < ep, expo, 0.0), -1, keepdims=True)
    high = gates.astype(BF16).astype(F32)
    ext = jnp.where(spot < ep, high, gates - high).astype(BF16)
    for part in (0, 2):
        xg[part, d, :, quart:quart + HEAD] = jnp.zeros((rows, HEAD), BF16)
        xg[part, d, :, quart:quart + 2 * ep] = ext

    def piece(q, src):
        return xg.at[2 * c + q, src] if q == 0 else xg.at[2 * c + q, src, :, 0:quart]

    moves = {}
    sib = []
    for q in range(2):
        for way in range(2):
            blk = piece(q, d)
            moves[way, q, 1] = send(blk, blk, x_s.at[way, q, 1], x_r.at[way, q, 1], dev=ahead[way])
    for st in range(1, hops + 1):
        for q in range(2):
            for way in range(2):
                top = limit(way, q)
                if st > top:
                    continue
                moves[way, q, st].wait_recv()
                blk = piece(q, origin(way, st))
                if st < top:
                    moves[way, q, st + 1] = send(
                        blk, blk, x_s.at[way, q, st + 1], x_r.at[way, q, st + 1], dev=ahead[way]
                    )
                sib.append(send(blk, blk, xs_s.at[way, q, st], xs_r.at[way, q, st], tp=1 - c))
    for cp in sib:
        cp.wait_recv()
    pending += list(moves.values()) + sib

    local[3].wait()
    local[4].wait()
    local[5].wait()
    mine = lax.rem(d, experts)

    @pl.loop(0, n, step=blocks)
    def _(j0):
        gt = jnp.zeros((mrows, wg.shape[1]), F32)
        up = gt
        for part in range(4):
            x = xg[part, pl.ds(j0, blocks), :, 0:quart].reshape(mrows, quart)
            at = slice(part * quart, (part + 1) * quart)
            gt = gt + jnp.dot(x, wg[at, :], preferred_element_type=F32)
            up = up + jnp.dot(x, wu[at, :], preferred_element_type=F32)
        act[pl.ds(j0, blocks)] = (
            (gt / (1.0 + jnp.exp(-gt)) * up).astype(BF16).reshape(blocks, rows, act.shape[2])
        )

    def expert_out(j0, start):
        e = xg[0, pl.ds(j0, blocks), :, quart:quart + HEAD].reshape(mrows, HEAD).astype(F32)
        ln = lax.broadcasted_iota(jnp.int32, (mrows, HEAD), 1)
        w = jnp.sum(jnp.where((ln == mine) | (ln == mine + ep), e, 0.0), -1, keepdims=True)
        x = act[pl.ds(j0, blocks)].reshape(mrows, act.shape[2])
        at = pl.ds(pl.multiple_of(start, quart), quart)
        return (jnp.dot(x, wd[:, at], preferred_element_type=F32) * w).reshape(blocks, rows, quart)

    pair = []
    for q in range(2):
        @pl.loop(0, n, step=blocks)
        def _(j0):
            ysib[q, pl.ds(j0, blocks)] = expert_out(j0, (1 - c) * half + q * quart).astype(BF16)

        pair.append(send(ysib.at[q], yin.at[q], y_s.at[q], y_r.at[q], tp=1 - c))

    moves = {}

    def own_part(q, j):
        return yacc[q, j] + yin[q, j].astype(F32)

    def pass_on(way, q, st, value):
        sbuf[way, q, st] = value.astype(BF16)
        moves[way, q, st] = send(
            sbuf.at[way, q, st], rbuf.at[way, q, st], m_s.at[way, q, st], m_r.at[way, q, st], dev=ahead[way]
        )

    for q in range(2):
        @pl.loop(0, n, step=blocks)
        def _(j0):
            yacc[q, pl.ds(j0, blocks)] = expert_out(j0, c * half + q * quart)

        pair[q].wait_recv()
        for way in range(2):
            pass_on(way, q, 1, own_part(q, origin(1 - way, limit(way, q))))
    total = [
        h1[:, pl.ds(pl.multiple_of(c * half + q * quart, quart), quart)] + own_part(q, d) for q in range(2)
    ]
    for st in range(1, hops + 1):
        for q in range(2):
            for way in range(2):
                top = limit(way, q)
                if st > top:
                    continue
                moves[way, q, st].wait_recv()
                got = rbuf[way, q, st].astype(F32)
                if st == top:
                    total[q] = total[q] + got
                else:
                    pass_on(way, q, st + 1, got + own_part(q, origin(1 - way, top - st)))
    for q in range(2):
        out_ref[:, q * quart:(q + 1) * quart] = total[q].astype(BF16)
    pending += pair + list(moves.values())
    for cp in pending:
        cp.wait_send()


def shards(
    n, h_in, query, key_cache, cached_value_rows, fresh_token_key, fresh_token_value,
    lengths, routes, w_out, gain, router_weight, w_gate, w_up, w_down,
):
    rows, width = h_in.shape
    experts = router_weight.shape[1]
    ep = -(-experts // 16) * 16
    half = width // 2
    kvh = fresh_token_key.shape[1] // HEAD
    heads = query.shape[1] // HEAD
    per = heads // kvh
    cw = w_out.shape[1]
    ff = w_gate.shape[2]
    hops = n // 2
    quart = half // 2
    slots = key_cache.shape[1]
    vm = pl.BlockSpec(memory_space=pltpu.VMEM)
    anyw = pl.BlockSpec(memory_space=pl.ANY)
    dma = pltpu.SemaphoreType.DMA
    return pl.pallas_call(
        functools.partial(layer_kernel, n, experts),
        out_shape=jax.ShapeDtypeStruct((rows, half), BF16),
        in_specs=[pl.BlockSpec(memory_space=pltpu.SMEM)] * 2 + [vm] * 6 + [anyw] * 6,
        out_specs=vm,
        scratch_shapes=[
            pltpu.VMEM(key_cache.shape, BF16),
            pltpu.VMEM(cached_value_rows.shape, BF16),
            pltpu.VMEM(w_out.shape, BF16),
            pltpu.VMEM(w_gate.shape[1:], BF16),
            pltpu.VMEM(w_up.shape[1:], BF16),
            pltpu.VMEM(w_down.shape[1:], BF16),
            pltpu.VMEM((2 * ep, width), BF16),
            pltpu.VMEM((rows * heads, HEAD), F32),
            pltpu.VMEM((kvh, rows, HEAD), F32),
            pltpu.VMEM((kvh, rows, HEAD), F32),
            pltpu.VMEM((rows * per, slots), F32),
            pltpu.VMEM((rows * per, HEAD), F32),
            pltpu.VMEM((rows * per, slots), BF16),
            pltpu.VMEM((rows * per, HEAD), F32),
            pltpu.VMEM((kvh, n, rows, per * HEAD), BF16),
            pltpu.VMEM((n, rows, cw), BF16),
            pltpu.VMEM((2, n, rows, cw), BF16),
            pltpu.VMEM((rows, width), F32),
            pltpu.VMEM((4, n, rows, quart + HEAD), BF16),
            pltpu.VMEM((n, rows, ff), BF16),
            pltpu.VMEM((2, n, rows, quart), BF16),
            pltpu.VMEM((2, n, rows, quart), BF16),
            pltpu.VMEM((2, n, rows, quart), F32),
            pltpu.VMEM((2, 2, hops + 1, rows, quart), BF16),
            pltpu.VMEM((2, 2, hops + 1, rows, quart), BF16),
            dma((6,)),
            dma((2, kvh, hops + 1)), dma((2, kvh, hops + 1)),
            dma((n,)), dma((n,)), dma((n,)), dma((n,)),
            dma((2, 2, hops + 1)), dma((2, 2, hops + 1)), dma((2, 2, hops + 1)), dma((2, 2, hops + 1)),
            dma((2,)), dma((2,)), dma((2, 2, hops + 1)), dma((2, 2, hops + 1)),
        ],
        compiler_params=pltpu.CompilerParams(
            collective_id=0, has_side_effects=True, vmem_limit_bytes=60 * 1024 * 1024
        ),
    )(
        lengths, routes.T, h_in, query, fresh_token_key, fresh_token_value,
        gain.reshape(-1, HEAD), router_weight.T,
        key_cache, cached_value_rows, w_out, w_gate, w_up, w_down,
    )


def solution(mesh):
    placed = (
        P(("groups", "dev"), None),
        P(("groups", "dev"), "tp"),
        P(("groups", "dev"), None, "tp"),
        P(("groups", "dev"), None, "tp"),
        P(("groups", "dev"), "tp"),
        P(("groups", "dev"), "tp"),
        P(("groups", "dev")),
        P(("groups", "dev"), None),
        P("tp", "dev"),
        P(),
        P(),
        P("dev", None, "tp"),
        P("dev", None, "tp"),
        P("dev", "tp", None),
    )
    return jax.shard_map(
        functools.partial(shards, mesh.shape["dev"]),
        mesh=mesh, in_specs=placed, out_specs=P(("groups", "dev"), "tp"), check_vma=False,
    )
```

```python
import functools
import math

import jax
import jax.numpy as jnp
from jax import lax
from jax.experimental import pallas as pl
from jax.experimental.pallas import tpu as pltpu
from jax.sharding import PartitionSpec as P

HEAD = 128
EPS = 1e-06
F32 = jnp.float32
BF16 = jnp.bfloat16
NT = (((1,), (1,)), ((), ()))


def layer_kernel(
    n, experts,
    len_ref, routes_ref, h_ref, q_ref, fk_ref, fv_ref, gain_ref, rw_ref,
    kc_hbm, vc_hbm, wo_hbm, wg_hbm, wu_hbm, wd_hbm,
    out_ref,
    kc, vc, wo, wg, wu, wd, rw,
    qs, fkf, fvf, sc, pn, pw, ob,
    eb, he, ag, pacc, pin, hg, h1, x2s, wrow, act, ysib, yin, yacc, tbuf, tin, sbuf, zin, din,
    lsem, e_s, e_r, a_s, a_r, af_s, af_r, pp_s, pp_r, hd_s, hd_r, hz_s, hz_r, hf_s, hf_r, hs_s, hs_r,
    y_s, y_r, t_s, t_r, z_s, z_r, m_s, m_r,
):
    d = lax.axis_index("dev")
    c = lax.axis_index("tp")
    hops = n // 2
    rows = q_ref.shape[0]
    width = h_ref.shape[1]
    half = width // 2
    quart = half // 2
    kvh = fk_ref.shape[1] // HEAD
    heads = q_ref.shape[1] // HEAD
    per = heads // kvh
    kpart = per * HEAD
    cw = wo.shape[1]
    ep = rw.shape[0]
    blocks = min(n, 128 // rows)
    mrows = blocks * rows

    cols = hops
    a = lax.div(d, 2)
    b = lax.rem(d, 2)
    twin = a * 2 + 1 - b

    def up(k, side=0):
        return lax.rem(a + k, cols) * 2 + (1 - b if side else b)

    def down(k, side=0):
        return lax.rem(a + cols - k, cols) * 2 + (1 - b if side else b)

    local = [
        pltpu.make_async_copy(src, dst, lsem.at[i])
        for i, (src, dst) in enumerate(
            [(kc_hbm, kc), (vc_hbm, vc), (wo_hbm, wo), (wg_hbm.at[0], wg), (wu_hbm.at[0], wu), (wd_hbm.at[0], wd)]
        )
    ]
    local[0].start()
    local[1].start()

    barrier = pltpu.get_barrier_semaphore()
    for k in range(1, n):
        pl.semaphore_signal(
            barrier, inc=1, device_id={"dev": lax.rem(d + k, n)}, device_id_type=pl.DeviceIdType.MESH
        )
    pl.semaphore_signal(barrier, inc=1, device_id={"tp": 1 - c}, device_id_type=pl.DeviceIdType.MESH)

    def send(src, dst, ssem, rsem, **to):
        cp = pltpu.make_async_remote_copy(
            src_ref=src, dst_ref=dst, send_sem=ssem, recv_sem=rsem,
            device_id=to, device_id_type=pl.DeviceIdType.MESH,
        )
        cp.start()
        return cp

    pending = []

    for hh in range(heads):
        qs[pl.ds(hh, rows, stride=heads), :] = q_ref[:, hh * HEAD:(hh + 1) * HEAD].astype(F32)
    for g in range(kvh):
        fkf[g] = fk_ref[:, g * HEAD:(g + 1) * HEAD].astype(F32)
        fvf[g] = fv_ref[:, g * HEAD:(g + 1) * HEAD].astype(F32)
    rw[...] = jnp.zeros(rw.shape, BF16)
    rw[0:experts, :] = rw_ref[...]
    spot = lax.broadcasted_iota(jnp.int32, (rows, HEAD), 1)
    line = lax.broadcasted_iota(jnp.int32, (rows, HEAD), 0)
    chosen = jnp.zeros((rows, HEAD), F32)
    for k in range(routes_ref.shape[0]):
        named = jnp.zeros((rows, HEAD), jnp.int32)
        for r in range(rows):
            named = jnp.where(line == r, routes_ref[k, r], named)
        chosen = jnp.where(spot == named, 1.0, chosen)
    for j in range(n):
        eb[j, :, 0:cw] = h_ref[:, j * cw:(j + 1) * cw]
        eb[j, :, cw:cw + HEAD] = chosen.astype(BF16)
    factor = 1.0 / math.sqrt(HEAD)
    slots = kc.shape[1]
    lane = lax.broadcasted_iota(jnp.int32, (per, slots), 1)
    step = 4
    cuts = 2
    chunk = 128
    early = []
    first = {}
    for g in range(kvh):
        if g == 0:
            local[0].wait()
            local[2].start()

        @pl.loop(0, rows, step=step)
        def _(r0):
            for i in range(step):
                r = r0 + i
                live = lane < len_ref[r]
                q = qs[pl.ds(pl.multiple_of(r * heads + g * per, per), per), :]
                at = pl.ds(pl.multiple_of(r * per, per), per)
                s = lax.dot_general(
                    q.astype(BF16), kc[r, :, g * HEAD:(g + 1) * HEAD], NT, preferred_element_type=F32
                )
                sc[at, :] = jnp.where(live, s * factor, -1e30)
                pn[at, :] = q * fkf[g, pl.ds(r, 1), :]

        if g == 0:
            pl.semaphore_wait(barrier, n)
            for k in range(1, n):
                j = lax.rem(d + k, n)
                early.append(send(eb.at[j], he.at[d], e_s.at[k], e_r.at[k], dev=j))
            he[d] = eb[d]

        @pl.loop(0, rows * per, step=chunk)
        def _(r0):
            at = pl.ds(pl.multiple_of(r0, chunk), chunk)
            s = sc[at, :]
            sn = jnp.sum(pn[at, :], -1, keepdims=True) * factor
            m = jnp.maximum(jnp.max(s, -1, keepdims=True), sn)
            p = jnp.exp(s - m)
            en = jnp.exp(sn - m)
            tot = jnp.sum(p, -1, keepdims=True) + en
            pw[at, :] = (p / tot).astype(BF16)
            pn[at, :] = jnp.broadcast_to((en / tot).astype(BF16).astype(F32), (chunk, HEAD))

        if g == 0:
            local[1].wait()
            for i in (3, 4, 5):
                local[i].start()

        @pl.loop(0, rows, step=step)
        def _(r0):
            for i in range(step):
                r = r0 + i
                at = pl.ds(pl.multiple_of(r * per, per), per)
                o = jnp.dot(pw[at, :], vc[r, :, g * HEAD:(g + 1) * HEAD], preferred_element_type=F32)
                ob[at, :] = o + pn[at, :] * fvf[g, pl.ds(r, 1), :]

        for u in range(cuts):
            w = g * cuts + u
            for hh in range(per // cuts):
                ag[w, d, :, hh * HEAD:(hh + 1) * HEAD] = ob[
                    pl.ds(u * (per // cuts) + hh, rows, stride=per), :
                ].astype(BF16)
            blk = ag.at[w, d]
            for k in range(1, cols):
                first[w, k] = send(blk, blk, a_s.at[w, k], a_r.at[w, k], dev=up(k))
            first[w, 0] = send(blk, blk, af_s.at[w, 0], af_r.at[w, 0], dev=twin)
    pending += early
    fwd = {}
    for w in range(kvh * cuts):
        for k in range(1, cols):
            first[w, k].wait_recv()
            blk = ag.at[w, down(k)]
            fwd[w, k] = send(blk, blk, af_s.at[w, k], af_r.at[w, k], dev=twin)
    for w in range(kvh * cuts):
        first[w, 0].wait_recv()
        for k in range(1, cols):
            fwd[w, k].wait_recv()
    pending += list(first.values()) + list(fwd.values())
    local[2].wait()
    kpart = kpart // cuts

    @pl.loop(0, n, step=blocks)
    def _(j0):
        y = jnp.zeros((mrows, cw), F32)
        for w in range(kvh * cuts):
            x = ag[w, pl.ds(j0, blocks)].reshape(mrows, kpart)
            y = y + jnp.dot(x, wo[w * kpart:(w + 1) * kpart, :], preferred_element_type=F32)
        pacc[pl.ds(j0, blocks)] = y.reshape(blocks, rows, cw)

    swap = send(pacc.at[pl.ds((1 - c) * hops, hops)], pin, pp_s, pp_r, tp=1 - c)
    for k in range(1, n):
        early[k - 1].wait_recv()
    swap.wait_recv()
    pending.append(swap)
    part = hops // 2

    def rows_of(core, q):
        return pl.ds(core * hops + q * part, part)

    for q in range(2):
        at = rows_of(c, q)
        hg[d, at] = (
            pacc[at] + pin[q * part:(q + 1) * part] + he[at, :, 0:cw].astype(F32)
        ).astype(BF16)
    one = hg.at[d, rows_of(c, 0)]
    two = hg.at[d, rows_of(c, 1)]
    zs = {}
    ds = {}
    for k in range(1, cols):
        zs[k] = send(one, one, hz_s.at[k], hz_r.at[k], dev=up(k))
    zs[0] = send(one, one, hf_s.at[0], hf_r.at[0], dev=twin)
    for k in range(1, n):
        ds[k] = send(two, two, hd_s.at[k], hd_r.at[k], dev=lax.rem(d + k, n))
    sib = [
        send(hg.at[d, rows_of(c, q)], hg.at[d, rows_of(c, q)], hs_s.at[q, 0], hs_r.at[q, 0], tp=1 - c)
        for q in range(2)
    ]

    def to_sibling(q, i, src):
        blk = hg.at[src, rows_of(c, q)]
        sib.append(send(blk, blk, hs_s.at[q, i], hs_r.at[q, i], tp=1 - c))

    hf = {}
    for k in range(1, cols):
        zs[k].wait_recv()
        blk = hg.at[down(k), rows_of(c, 0)]
        hf[k] = send(blk, blk, hf_s.at[k], hf_r.at[k], dev=twin)
        to_sibling(0, k, down(k))
    zs[0].wait_recv()
    to_sibling(0, cols, twin)
    for k in range(1, n):
        ds[k].wait_recv()
        to_sibling(1, k, lax.rem(d + n - k, n))
    for k in range(1, cols):
        hf[k].wait_recv()
        to_sibling(0, cols + k, down(k, 1))
    for cp in sib:
        cp.wait_recv()
    pending += list(zs.values()) + list(ds.values()) + list(hf.values()) + sib

    mine = lax.rem(d, experts)
    gain = gain_ref[...].astype(F32)
    lanes = cw // HEAD

    @pl.loop(0, n, step=blocks)
    def _(j0):
        ss = jnp.zeros((mrows, HEAD), F32)
        for t in range(n):
            for i in range(lanes):
                v = hg[t, pl.ds(j0, blocks), :, i * HEAD:(i + 1) * HEAD].reshape(mrows, HEAD).astype(F32)
                ss = ss + v * v
        scale = lax.rsqrt(jnp.sum(ss, -1, keepdims=True) / width + EPS)
        here = pl.ds(pl.multiple_of(j0 * rows, mrows), mrows)
        for t in range(n):
            for i in range(lanes):
                v = hg[t, pl.ds(j0, blocks), :, i * HEAD:(i + 1) * HEAD].reshape(mrows, HEAD).astype(F32)
                at = t * lanes + i
                x2s[here, at * HEAD:(at + 1) * HEAD] = (v * scale * gain[at:at + 1, :]).astype(BF16)
        logits = lax.dot_general(x2s[here, :], rw[...], NT, preferred_element_type=F32)
        named = he[pl.ds(j0, blocks), :, cw:cw + HEAD].reshape(mrows, HEAD)[:, 0:ep].astype(F32) > 0.5
        expo = jnp.where(named, jnp.exp(logits), 0.0)
        spot = lax.broadcasted_iota(jnp.int32, (mrows, ep), 1)
        top = jnp.sum(jnp.where(spot == mine, expo, 0.0), -1, keepdims=True)
        wrow[here, :] = jnp.broadcast_to(top / jnp.sum(expo, -1, keepdims=True), (mrows, HEAD))

    for i in range(hops):
        h1[:, i * cw:(i + 1) * cw] = hg[c * hops + i, d].astype(F32)

    local[3].wait()
    local[4].wait()
    local[5].wait()

    @pl.loop(0, n, step=blocks)
    def _(j0):
        x = x2s[pl.ds(pl.multiple_of(j0 * rows, mrows), mrows), :]
        gt = jnp.dot(x, wg[...], preferred_element_type=F32)
        up_ = jnp.dot(x, wu[...], preferred_element_type=F32)
        act[pl.ds(j0, blocks)] = (
            (gt / (1.0 + jnp.exp(-gt)) * up_).astype(BF16).reshape(blocks, rows, act.shape[2])
        )

    def expert_out(j0, start):
        w = wrow[pl.ds(pl.multiple_of(j0 * rows, mrows), mrows), 0:1]
        x = act[pl.ds(j0, blocks)].reshape(mrows, act.shape[2])
        at = pl.ds(pl.multiple_of(start, quart), quart)
        return (jnp.dot(x, wd[:, at], preferred_element_type=F32) * w).reshape(blocks, rows, quart)

    pair = []
    for q in range(2):
        @pl.loop(0, n, step=blocks)
        def _(j0):
            ysib[q, pl.ds(j0, blocks)] = expert_out(j0, (1 - c) * half + q * quart).astype(BF16)

        pair.append(send(ysib.at[q], yin.at[q], y_s.at[q], y_r.at[q], tp=1 - c))

    def own_part(q, j):
        return yacc[q, j] + yin[q, j].astype(F32)

    def compute(q):
        @pl.loop(0, n, step=blocks)
        def _(j0):
            yacc[q, pl.ds(j0, blocks)] = expert_out(j0, c * half + q * quart)

        pair[q].wait_recv()

    compute(0)
    ts = {}
    for k in range(cols - 1, -1, -1):
        tbuf[k] = own_part(0, up(k, 1)).astype(BF16)
        ts[k] = send(tbuf.at[k], tin.at[k], t_s.at[k], t_r.at[k], dev=twin)
    compute(1)
    ds = {}
    for k in range(1, n):
        j = lax.rem(d + k, n)
        sbuf[k] = own_part(1, j).astype(BF16)
        ds[k] = send(sbuf.at[k], din.at[k], m_s.at[k], m_r.at[k], dev=j)
    zs = {}
    for k in range(cols - 1, 0, -1):
        ts[k].wait_recv()
        tbuf[cols + k] = (own_part(0, up(k)) + tin[k].astype(F32)).astype(BF16)
        zs[k] = send(tbuf.at[cols + k], zin.at[k], z_s.at[k], z_r.at[k], dev=up(k))
    total = [h1[:, q * quart:(q + 1) * quart] + own_part(q, d) for q in range(2)]
    ts[0].wait_recv()
    total[0] = total[0] + tin[0].astype(F32)
    for k in range(1, n):
        ds[k].wait_recv()
        total[1] = total[1] + din[k].astype(F32)
    for k in range(cols - 1, 0, -1):
        zs[k].wait_recv()
        total[0] = total[0] + zin[k].astype(F32)
    for q in range(2):
        out_ref[:, q * quart:(q + 1) * quart] = total[q].astype(BF16)
    pending += pair + list(ts.values()) + list(ds.values()) + list(zs.values())
    for cp in pending:
        cp.wait_send()


def shards(
    n, h_in, query, key_cache, cached_value_rows, fresh_token_key, fresh_token_value,
    lengths, routes, w_out, gain, router_weight, w_gate, w_up, w_down,
):
    rows, width = h_in.shape
    experts = router_weight.shape[1]
    ep = -(-experts // 16) * 16
    half = width // 2
    kvh = fresh_token_key.shape[1] // HEAD
    heads = query.shape[1] // HEAD
    per = heads // kvh
    cw = w_out.shape[1]
    ff = w_gate.shape[2]
    hops = n // 2
    quart = half // 2
    slots = key_cache.shape[1]
    vm = pl.BlockSpec(memory_space=pltpu.VMEM)
    anyw = pl.BlockSpec(memory_space=pl.ANY)
    dma = pltpu.SemaphoreType.DMA
    return pl.pallas_call(
        functools.partial(layer_kernel, n, experts),
        out_shape=jax.ShapeDtypeStruct((rows, half), BF16),
        in_specs=[pl.BlockSpec(memory_space=pltpu.SMEM)] * 2 + [vm] * 6 + [anyw] * 6,
        out_specs=vm,
        scratch_shapes=[
            pltpu.VMEM(key_cache.shape, BF16),
            pltpu.VMEM(cached_value_rows.shape, BF16),
            pltpu.VMEM(w_out.shape, BF16),
            pltpu.VMEM(w_gate.shape[1:], BF16),
            pltpu.VMEM(w_up.shape[1:], BF16),
            pltpu.VMEM(w_down.shape[1:], BF16),
            pltpu.VMEM((-(-experts // 16) * 16, width), BF16),
            pltpu.VMEM((rows * heads, HEAD), F32),
            pltpu.VMEM((kvh, rows, HEAD), F32),
            pltpu.VMEM((kvh, rows, HEAD), F32),
            pltpu.VMEM((rows * per, slots), F32),
            pltpu.VMEM((rows * per, HEAD), F32),
            pltpu.VMEM((rows * per, slots), BF16),
            pltpu.VMEM((rows * per, HEAD), F32),
            pltpu.VMEM((n, rows, cw + HEAD), BF16),
            pltpu.VMEM((n, rows, cw + HEAD), BF16),
            pltpu.VMEM((2 * kvh, n, rows, per * HEAD // 2), BF16),
            pltpu.VMEM((n, rows, cw), F32),
            pltpu.VMEM((hops, rows, cw), F32),
            pltpu.VMEM((n, n, rows, cw), BF16),
            pltpu.VMEM((rows, half), F32),
            pltpu.VMEM((n * rows, width), BF16),
            pltpu.VMEM((n * rows, HEAD), F32),
            pltpu.VMEM((n, rows, ff), BF16),
            pltpu.VMEM((2, n, rows, quart), BF16),
            pltpu.VMEM((2, n, rows, quart), BF16),
            pltpu.VMEM((2, n, rows, quart), F32),
            pltpu.VMEM((2 * hops, rows, quart), BF16),
            pltpu.VMEM((hops, rows, quart), BF16),
            pltpu.VMEM((n, rows, quart), BF16),
            pltpu.VMEM((hops, rows, quart), BF16),
            pltpu.VMEM((n, rows, quart), BF16),
            dma((6,)), dma((n,)), dma((n,)),
            dma((2 * kvh, hops)), dma((2 * kvh, hops)), dma((2 * kvh, hops)), dma((2 * kvh, hops)),
            dma, dma, dma((n,)), dma((n,)), dma((hops,)), dma((hops,)), dma((hops,)), dma((hops,)),
            dma((2, n)), dma((2, n)),
            dma((2,)), dma((2,)), dma((hops,)), dma((hops,)), dma((hops,)), dma((hops,)), dma((n,)), dma((n,)),
        ],
        compiler_params=pltpu.CompilerParams(
            collective_id=0, has_side_effects=True, vmem_limit_bytes=60 * 1024 * 1024
        ),
    )(
        lengths, routes.T, h_in, query, fresh_token_key, fresh_token_value,
        gain.reshape(-1, HEAD), router_weight.T,
        key_cache, cached_value_rows, w_out, w_gate, w_up, w_down,
    )


def solution(mesh):
    placed = (
        P(("groups", "dev"), None),
        P(("groups", "dev"), "tp"),
        P(("groups", "dev"), None, "tp"),
        P(("groups", "dev"), None, "tp"),
        P(("groups", "dev"), "tp"),
        P(("groups", "dev"), "tp"),
        P(("groups", "dev")),
        P(("groups", "dev"), None),
        P("tp", "dev"),
        P(),
        P(),
        P("dev", None, "tp"),
        P("dev", None, "tp"),
        P("dev", "tp", None),
    )
    return jax.shard_map(
        functools.partial(shards, mesh.shape["dev"]),
        mesh=mesh, in_specs=placed, out_specs=P(("groups", "dev"), "tp"), check_vma=False,
    )
```

```python
import functools
import math

import jax
import jax.numpy as jnp
from jax import lax
from jax.experimental import pallas as pl
from jax.experimental.pallas import tpu as pltpu
from jax.sharding import PartitionSpec as P

HEAD = 128
EPS = 1e-06
F32 = jnp.float32
BF16 = jnp.bfloat16
NT = (((1,), (1,)), ((), ()))


def layer_kernel(
    n, experts,
    len_ref, routes_ref, h_ref, q_ref, fk_ref, fv_ref, gain_ref, rw_ref,
    kc_hbm, vc_hbm, wo_hbm, wg_hbm, wu_hbm, wd_hbm,
    out_ref,
    kc, vc, wo, wg, wu, wd, rw,
    qs, fkf, fvf, sc, pn, pw, ob,
    eb, he, ag, pacc, pin, hg, h1, x2s, wrow, act, ysib, yin, yacc, tbuf, tin, sbuf, zin, din,
    lsem, e_s, e_r, a_s, a_r, pp_s, pp_r, hd_s, hd_r, hz_s, hz_r, hf_s, hf_r, hs_s, hs_r,
    y_s, y_r, t_s, t_r, z_s, z_r, m_s, m_r,
):
    d = lax.axis_index("dev")
    c = lax.axis_index("tp")
    hops = n // 2
    rows = q_ref.shape[0]
    width = h_ref.shape[1]
    half = width // 2
    quart = half // 2
    kvh = fk_ref.shape[1] // HEAD
    heads = q_ref.shape[1] // HEAD
    per = heads // kvh
    kpart = per * HEAD
    cw = wo.shape[1]
    ep = rw.shape[0]
    blocks = min(n, 128 // rows)
    mrows = blocks * rows

    cols = hops
    a = lax.div(d, 2)
    b = lax.rem(d, 2)
    twin = a * 2 + 1 - b

    def up(k, side=0):
        return lax.rem(a + k, cols) * 2 + (1 - b if side else b)

    def down(k, side=0):
        return lax.rem(a + cols - k, cols) * 2 + (1 - b if side else b)

    pos = (1 - b) * a + b * (n - 1 - a)

    def at_pos(k):
        p = lax.rem(pos + (k % n), n)
        back = lax.div(p, hops)
        return (1 - back) * 2 * p + back * (2 * (n - 1 - p) + 1)

    ahead = (at_pos(1), at_pos(-1))

    def limit(way, w):
        return hops if way == w % 2 else hops - 1

    local = [
        pltpu.make_async_copy(src, dst, lsem.at[i])
        for i, (src, dst) in enumerate(
            [(kc_hbm, kc), (vc_hbm, vc), (wo_hbm, wo), (wg_hbm.at[0], wg), (wu_hbm.at[0], wu), (wd_hbm.at[0], wd)]
        )
    ]
    local[0].start()
    local[1].start()

    barrier = pltpu.get_barrier_semaphore()
    for k in range(1, n):
        pl.semaphore_signal(
            barrier, inc=1, device_id={"dev": lax.rem(d + k, n)}, device_id_type=pl.DeviceIdType.MESH
        )
    pl.semaphore_signal(barrier, inc=1, device_id={"tp": 1 - c}, device_id_type=pl.DeviceIdType.MESH)

    def send(src, dst, ssem, rsem, **to):
        cp = pltpu.make_async_remote_copy(
            src_ref=src, dst_ref=dst, send_sem=ssem, recv_sem=rsem,
            device_id=to, device_id_type=pl.DeviceIdType.MESH,
        )
        cp.start()
        return cp

    pending = []

    for hh in range(heads):
        qs[pl.ds(hh, rows, stride=heads), :] = q_ref[:, hh * HEAD:(hh + 1) * HEAD].astype(F32)
    for g in range(kvh):
        fkf[g] = fk_ref[:, g * HEAD:(g + 1) * HEAD].astype(F32)
        fvf[g] = fv_ref[:, g * HEAD:(g + 1) * HEAD].astype(F32)
    rw[...] = jnp.zeros(rw.shape, BF16)
    rw[0:experts, :] = rw_ref[...]
    spot = lax.broadcasted_iota(jnp.int32, (rows, HEAD), 1)
    line = lax.broadcasted_iota(jnp.int32, (rows, HEAD), 0)
    chosen = jnp.zeros((rows, HEAD), F32)
    for k in range(routes_ref.shape[0]):
        named = jnp.zeros((rows, HEAD), jnp.int32)
        for r in range(rows):
            named = jnp.where(line == r, routes_ref[k, r], named)
        chosen = jnp.where(spot == named, 1.0, chosen)
    for j in range(n):
        eb[j, :, 0:cw] = h_ref[:, j * cw:(j + 1) * cw]
        eb[j, :, cw:cw + HEAD] = chosen.astype(BF16)
    factor = 1.0 / math.sqrt(HEAD)
    slots = kc.shape[1]
    lane = lax.broadcasted_iota(jnp.int32, (per, slots), 1)
    step = rows
    cuts = 2
    chunk = 128
    early = []
    first = {}
    for g in range(kvh):
        if g == 0:
            local[0].wait()
            local[2].start()

        @pl.loop(0, rows, step=step)
        def _(r0):
            for i in range(step):
                r = r0 + i
                live = lane < len_ref[r]
                q = qs[pl.ds(pl.multiple_of(r * heads + g * per, per), per), :]
                at = pl.ds(pl.multiple_of(r * per, per), per)
                s = lax.dot_general(
                    q.astype(BF16), kc[r, :, g * HEAD:(g + 1) * HEAD], NT, preferred_element_type=F32
                )
                sc[at, :] = jnp.where(live, s * factor, -1e30)
                pn[at, :] = q * fkf[g, pl.ds(r, 1), :]

        if g == 0:
            pl.semaphore_wait(barrier, n)
            for k in range(1, n):
                j = lax.rem(d + k, n)
                early.append(send(eb.at[j], he.at[d], e_s.at[k], e_r.at[k], dev=j))
            he[d] = eb[d]

        @pl.loop(0, rows * per, step=chunk)
        def _(r0):
            at = pl.ds(pl.multiple_of(r0, chunk), chunk)
            s = sc[at, :]
            sn = jnp.sum(pn[at, :], -1, keepdims=True) * factor
            m = jnp.maximum(jnp.max(s, -1, keepdims=True), sn)
            p = jnp.exp(s - m)
            en = jnp.exp(sn - m)
            tot = jnp.sum(p, -1, keepdims=True) + en
            pw[at, :] = (p / tot).astype(BF16)
            pn[at, :] = jnp.broadcast_to((en / tot).astype(BF16).astype(F32), (chunk, HEAD))

        if g == 0:
            local[1].wait()
            for i in (3, 4, 5):
                local[i].start()

        @pl.loop(0, rows, step=step)
        def _(r0):
            for i in range(step):
                r = r0 + i
                at = pl.ds(pl.multiple_of(r * per, per), per)
                o = jnp.dot(pw[at, :], vc[r, :, g * HEAD:(g + 1) * HEAD], preferred_element_type=F32)
                ob[at, :] = o + pn[at, :] * fvf[g, pl.ds(r, 1), :]

        for u in range(cuts):
            w = g * cuts + u
            for hh in range(per // cuts):
                ag[w, d, :, hh * HEAD:(hh + 1) * HEAD] = ob[
                    pl.ds(u * (per // cuts) + hh, rows, stride=per), :
                ].astype(BF16)
            blk = ag.at[w, d]
            for way in range(2):
                first[way, w, 1] = send(blk, blk, a_s.at[way, w, 1], a_r.at[way, w, 1], dev=ahead[way])
    pending += early
    for st in range(1, hops + 1):
        for w in range(kvh * cuts):
            for way in range(2):
                last = limit(way, w)
                if st <= last:
                    first[way, w, st].wait_recv()
                if st < last:
                    blk = ag.at[w, at_pos(-st if way == 0 else st)]
                    first[way, w, st + 1] = send(
                        blk, blk, a_s.at[way, w, st + 1], a_r.at[way, w, st + 1], dev=ahead[way]
                    )
    pending += list(first.values())
    local[2].wait()
    kpart = kpart // cuts

    @pl.loop(0, n, step=blocks)
    def _(j0):
        y = jnp.zeros((mrows, cw), F32)
        for w in range(kvh * cuts):
            x = ag[w, pl.ds(j0, blocks)].reshape(mrows, kpart)
            y = y + jnp.dot(x, wo[w * kpart:(w + 1) * kpart, :], preferred_element_type=F32)
        pacc[pl.ds(j0, blocks)] = y.reshape(blocks, rows, cw)

    swap = send(pacc.at[pl.ds((1 - c) * hops, hops)], pin, pp_s, pp_r, tp=1 - c)
    for k in range(1, n):
        early[k - 1].wait_recv()
    swap.wait_recv()
    pending.append(swap)
    part = hops // 2

    def rows_of(core, q):
        return pl.ds(core * hops + q * part, part)

    for q in range(2):
        at = rows_of(c, q)
        hg[d, at] = (
            pacc[at] + pin[q * part:(q + 1) * part] + he[at, :, 0:cw].astype(F32)
        ).astype(BF16)
    one = hg.at[d, rows_of(c, 0)]
    two = hg.at[d, rows_of(c, 1)]
    zs = {}
    ds = {}
    for k in range(1, cols):
        zs[k] = send(one, one, hz_s.at[k], hz_r.at[k], dev=up(k))
    zs[0] = send(one, one, hf_s.at[0], hf_r.at[0], dev=twin)
    for k in range(1, n):
        ds[k] = send(two, two, hd_s.at[k], hd_r.at[k], dev=lax.rem(d + k, n))
    sib = [
        send(hg.at[d, rows_of(c, q)], hg.at[d, rows_of(c, q)], hs_s.at[q, 0], hs_r.at[q, 0], tp=1 - c)
        for q in range(2)
    ]

    def to_sibling(q, i, src):
        blk = hg.at[src, rows_of(c, q)]
        sib.append(send(blk, blk, hs_s.at[q, i], hs_r.at[q, i], tp=1 - c))

    hf = {}
    for k in range(1, cols):
        zs[k].wait_recv()
        blk = hg.at[down(k), rows_of(c, 0)]
        hf[k] = send(blk, blk, hf_s.at[k], hf_r.at[k], dev=twin)
        to_sibling(0, k, down(k))
    zs[0].wait_recv()
    to_sibling(0, cols, twin)
    for k in range(1, n):
        ds[k].wait_recv()
        to_sibling(1, k, lax.rem(d + n - k, n))
    for k in range(1, cols):
        hf[k].wait_recv()
        to_sibling(0, cols + k, down(k, 1))
    for cp in sib:
        cp.wait_recv()
    pending += list(zs.values()) + list(ds.values()) + list(hf.values()) + sib

    mine = lax.rem(d, experts)
    gain = gain_ref[...].astype(F32)
    lanes = cw // HEAD

    @pl.loop(0, n, step=blocks)
    def _(j0):
        ss = jnp.zeros((mrows, HEAD), F32)
        for t in range(n):
            for i in range(lanes):
                v = hg[t, pl.ds(j0, blocks), :, i * HEAD:(i + 1) * HEAD].reshape(mrows, HEAD).astype(F32)
                ss = ss + v * v
        scale = lax.rsqrt(jnp.sum(ss, -1, keepdims=True) / width + EPS)
        here = pl.ds(pl.multiple_of(j0 * rows, mrows), mrows)
        for t in range(n):
            for i in range(lanes):
                v = hg[t, pl.ds(j0, blocks), :, i * HEAD:(i + 1) * HEAD].reshape(mrows, HEAD).astype(F32)
                at = t * lanes + i
                x2s[here, at * HEAD:(at + 1) * HEAD] = (v * scale * gain[at:at + 1, :]).astype(BF16)
        logits = lax.dot_general(x2s[here, :], rw[...], NT, preferred_element_type=F32)
        named = he[pl.ds(j0, blocks), :, cw:cw + HEAD].reshape(mrows, HEAD)[:, 0:ep].astype(F32) > 0.5
        expo = jnp.where(named, jnp.exp(logits), 0.0)
        spot = lax.broadcasted_iota(jnp.int32, (mrows, ep), 1)
        top = jnp.sum(jnp.where(spot == mine, expo, 0.0), -1, keepdims=True)
        wrow[here, :] = jnp.broadcast_to(top / jnp.sum(expo, -1, keepdims=True), (mrows, HEAD))

    for i in range(hops):
        h1[:, i * cw:(i + 1) * cw] = hg[c * hops + i, d].astype(F32)

    local[3].wait()
    local[4].wait()
    local[5].wait()

    @pl.loop(0, n, step=blocks)
    def _(j0):
        x = x2s[pl.ds(pl.multiple_of(j0 * rows, mrows), mrows), :]
        gt = jnp.dot(x, wg[...], preferred_element_type=F32)
        up_ = jnp.dot(x, wu[...], preferred_element_type=F32)
        act[pl.ds(j0, blocks)] = (
            (gt / (1.0 + jnp.exp(-gt)) * up_).astype(BF16).reshape(blocks, rows, act.shape[2])
        )

    def expert_out(j0, start):
        w = wrow[pl.ds(pl.multiple_of(j0 * rows, mrows), mrows), 0:1]
        x = act[pl.ds(j0, blocks)].reshape(mrows, act.shape[2])
        at = pl.ds(pl.multiple_of(start, quart), quart)
        return (jnp.dot(x, wd[:, at], preferred_element_type=F32) * w).reshape(blocks, rows, quart)

    pair = []
    for q in range(2):
        @pl.loop(0, n, step=blocks)
        def _(j0):
            ysib[q, pl.ds(j0, blocks)] = expert_out(j0, (1 - c) * half + q * quart).astype(BF16)

        pair.append(send(ysib.at[q], yin.at[q], y_s.at[q], y_r.at[q], tp=1 - c))

    def own_part(q, j):
        return yacc[q, j] + yin[q, j].astype(F32)

    def compute(q):
        @pl.loop(0, n, step=blocks)
        def _(j0):
            yacc[q, pl.ds(j0, blocks)] = expert_out(j0, c * half + q * quart)

        pair[q].wait_recv()

    compute(0)
    ts = {}
    for k in range(cols - 1, -1, -1):
        tbuf[k] = own_part(0, up(k, 1)).astype(BF16)
        ts[k] = send(tbuf.at[k], tin.at[k], t_s.at[k], t_r.at[k], dev=twin)
    compute(1)
    ds = {}
    for k in range(1, n):
        j = lax.rem(d + k, n)
        sbuf[k] = own_part(1, j).astype(BF16)
        ds[k] = send(sbuf.at[k], din.at[k], m_s.at[k], m_r.at[k], dev=j)
    zs = {}
    for k in range(cols - 1, 0, -1):
        ts[k].wait_recv()
        tbuf[cols + k] = (own_part(0, up(k)) + tin[k].astype(F32)).astype(BF16)
        zs[k] = send(tbuf.at[cols + k], zin.at[k], z_s.at[k], z_r.at[k], dev=up(k))
    total = [h1[:, q * quart:(q + 1) * quart] + own_part(q, d) for q in range(2)]
    ts[0].wait_recv()
    total[0] = total[0] + tin[0].astype(F32)
    for k in range(1, n):
        ds[k].wait_recv()
        total[1] = total[1] + din[k].astype(F32)
    for k in range(cols - 1, 0, -1):
        zs[k].wait_recv()
        total[0] = total[0] + zin[k].astype(F32)
    for q in range(2):
        out_ref[:, q * quart:(q + 1) * quart] = total[q].astype(BF16)
    pending += pair + list(ts.values()) + list(ds.values()) + list(zs.values())
    for cp in pending:
        cp.wait_send()


def shards(
    n, h_in, query, key_cache, cached_value_rows, fresh_token_key, fresh_token_value,
    lengths, routes, w_out, gain, router_weight, w_gate, w_up, w_down,
):
    rows, width = h_in.shape
    experts = router_weight.shape[1]
    ep = -(-experts // 16) * 16
    half = width // 2
    kvh = fresh_token_key.shape[1] // HEAD
    heads = query.shape[1] // HEAD
    per = heads // kvh
    cw = w_out.shape[1]
    ff = w_gate.shape[2]
    hops = n // 2
    quart = half // 2
    slots = key_cache.shape[1]
    vm = pl.BlockSpec(memory_space=pltpu.VMEM)
    anyw = pl.BlockSpec(memory_space=pl.ANY)
    dma = pltpu.SemaphoreType.DMA
    return pl.pallas_call(
        functools.partial(layer_kernel, n, experts),
        out_shape=jax.ShapeDtypeStruct((rows, half), BF16),
        in_specs=[pl.BlockSpec(memory_space=pltpu.SMEM)] * 2 + [vm] * 6 + [anyw] * 6,
        out_specs=vm,
        scratch_shapes=[
            pltpu.VMEM(key_cache.shape, BF16),
            pltpu.VMEM(cached_value_rows.shape, BF16),
            pltpu.VMEM(w_out.shape, BF16),
            pltpu.VMEM(w_gate.shape[1:], BF16),
            pltpu.VMEM(w_up.shape[1:], BF16),
            pltpu.VMEM(w_down.shape[1:], BF16),
            pltpu.VMEM((-(-experts // 16) * 16, width), BF16),
            pltpu.VMEM((rows * heads, HEAD), F32),
            pltpu.VMEM((kvh, rows, HEAD), F32),
            pltpu.VMEM((kvh, rows, HEAD), F32),
            pltpu.VMEM((rows * per, slots), F32),
            pltpu.VMEM((rows * per, HEAD), F32),
            pltpu.VMEM((rows * per, slots), BF16),
            pltpu.VMEM((rows * per, HEAD), F32),
            pltpu.VMEM((n, rows, cw + HEAD), BF16),
            pltpu.VMEM((n, rows, cw + HEAD), BF16),
            pltpu.VMEM((2 * kvh, n, rows, per * HEAD // 2), BF16),
            pltpu.VMEM((n, rows, cw), F32),
            pltpu.VMEM((hops, rows, cw), F32),
            pltpu.VMEM((n, n, rows, cw), BF16),
            pltpu.VMEM((rows, half), F32),
            pltpu.VMEM((n * rows, width), BF16),
            pltpu.VMEM((n * rows, HEAD), F32),
            pltpu.VMEM((n, rows, ff), BF16),
            pltpu.VMEM((2, n, rows, quart), BF16),
            pltpu.VMEM((2, n, rows, quart), BF16),
            pltpu.VMEM((2, n, rows, quart), F32),
            pltpu.VMEM((2 * hops, rows, quart), BF16),
            pltpu.VMEM((hops, rows, quart), BF16),
            pltpu.VMEM((n, rows, quart), BF16),
            pltpu.VMEM((hops, rows, quart), BF16),
            pltpu.VMEM((n, rows, quart), BF16),
            dma((6,)), dma((n,)), dma((n,)),
            dma((2, 2 * kvh, hops + 1)), dma((2, 2 * kvh, hops + 1)),
            dma, dma, dma((n,)), dma((n,)), dma((hops,)), dma((hops,)), dma((hops,)), dma((hops,)),
            dma((2, n)), dma((2, n)),
            dma((2,)), dma((2,)), dma((hops,)), dma((hops,)), dma((hops,)), dma((hops,)), dma((n,)), dma((n,)),
        ],
        compiler_params=pltpu.CompilerParams(
            collective_id=0, has_side_effects=True, vmem_limit_bytes=60 * 1024 * 1024
        ),
    )(
        lengths, routes.T, h_in, query, fresh_token_key, fresh_token_value,
        gain.reshape(-1, HEAD), router_weight.T,
        key_cache, cached_value_rows, w_out, w_gate, w_up, w_down,
    )


def solution(mesh):
    placed = (
        P(("groups", "dev"), None),
        P(("groups", "dev"), "tp"),
        P(("groups", "dev"), None, "tp"),
        P(("groups", "dev"), None, "tp"),
        P(("groups", "dev"), "tp"),
        P(("groups", "dev"), "tp"),
        P(("groups", "dev")),
        P(("groups", "dev"), None),
        P("tp", "dev"),
        P(),
        P(),
        P("dev", None, "tp"),
        P("dev", None, "tp"),
        P("dev", "tp", None),
    )
    return jax.shard_map(
        functools.partial(shards, mesh.shape["dev"]),
        mesh=mesh, in_specs=placed, out_specs=P(("groups", "dev"), "tp"), check_vma=False,
    )
```
